32 devices in a mesh: groups: 2 (over x), ep: 16 (over z, y, core).
Axes of the slice: x: 2, y: 2, z: 4, core: 2. Of those that a mesh axis runs over, the one named last changes fastest.
Arguments:
- tokens: bfloat16 [2048, 2048], P(('groups', 'ep')), parts along dimension 0, may hold values from -6 to 6
- expert_ids: int32 [2048, 8], P(('groups', 'ep')), parts along dimension 0, may hold values from 0 to 15, as said below
- gate_values: float32 [2048, 8], P(('groups', 'ep')), parts along dimension 0, may hold values from 0.1 to 1
- expert_weights: bfloat16 [32, 2048, 3072], P(('groups', 'ep')), parts along dimension 0, as said below
- home_slot: int32 [32], P('groups'), parts along dimension 0, may hold values from 0 to 15, as said below
- spare_expert: int32 [32], P('groups'), parts along dimension 0, may hold values from -1 to 15, as said below
Outputs:
- moe_out: bfloat16 [2048, 2048], P(('groups', 'ep')), parts along dimension 0
The draws below stay inside these ranges and needn't reach their ends.
There are 2 independent parts, one for each index of `groups`. The reference program is written for one: setup_inputs(seed, part) draws one part's arguments, and reference() takes and returns one part's arrays. A program takes and returns all parts, laid end to end along the dimension named above; each array names one. Nothing has to cross between parts.
Inputs may be any that keep to these rules, and one draw needn't show every extreme that they name: `expert_ids`: each row names 8 different experts. `home_slot`: a permutation of the experts. `spare_expert`: each expert is named a multiple of 3 times, at most 6, and some expert exactly 3 * 2 times; -1 stands in as many entries as the remainder of 16 divided by 3. `expert_weights`: the second slot of the device holding the k-th third of a split copy of expert e equals the matching gate, up and down columns (hidden units k * 256 to (k + 1) * 256 - 1) of e's home block.
All inputs are finite; a program needn't handle non-finite values.
Results may differ from the reference program's by a relative error of at most 0.0058.
Values may be sent and summed in bfloat16 or wider, within the bound.
A program may use at most 128 MiB of HBM per device.

```python
import jax
import jax.numpy as jnp
from jax import lax

D = 2048
FF = 768
TOP = 8
RMAX = 2
TOK_DEV = 64
EXPERTS = 16
TOKENS = 1024
CAP = 32
N_EP = 16


def placement(key):
    popular = jax.random.permutation(jax.random.fold_in(key, 7), EXPERTS).astype(jnp.int32)
    home = jax.random.permutation(jax.random.fold_in(key, 5), EXPERTS).astype(jnp.int32)
    copy_counts = jax.random.randint(jax.random.fold_in(key, 13), (EXPERTS,), 1, RMAX + 1, dtype=jnp.int32)
    copy_counts = copy_counts.at[0].set(RMAX)
    running = jnp.cumsum(copy_counts)
    positions = jnp.arange(EXPERTS, dtype=jnp.int32)
    copy_number = positions // 3
    hot_index = jnp.sum((running[None, :] <= copy_number[:, None]).astype(jnp.int32), axis=1)
    hot_index = jnp.minimum(hot_index, EXPERTS - 1).astype(jnp.int32)
    listed = jnp.where(positions < 3 * (EXPERTS // 3), popular[hot_index], -1).astype(jnp.int32)
    shuffled = jax.random.permutation(jax.random.fold_in(key, 17), EXPERTS).astype(jnp.int32)
    spare = jnp.zeros((EXPERTS,), jnp.int32).at[shuffled].set(listed)
    return (popular, home, spare.astype(jnp.int32))


def draw_home_slot(key, part):
    popular, home, spare = placement(key)
    return home


def draw_spare_expert(key, part):
    popular, home, spare = placement(key)
    return spare


def draw_expert_ids(key, part):
    popular, home, spare = placement(key)
    ranking = jnp.zeros((EXPERTS,), jnp.int32).at[popular].set(jnp.arange(EXPERTS, dtype=jnp.int32))
    lift_amount = 40 * jnp.maximum(0, 10 - ranking)
    scores = jax.random.randint(jax.random.fold_in(key, 11), (TOKENS, EXPERTS), 0, 1000, dtype=jnp.int32)
    scores = (scores + lift_amount[None, :]) * EXPERTS + jnp.arange(EXPERTS, dtype=jnp.int32)[None, :]
    return lax.top_k(scores, TOP)[1].astype(jnp.int32)


def draw_expert_weights(key, part):
    popular, home, spare = placement(key)
    width = 3 * FF
    third_width = FF // 3
    base = jax.random.truncated_normal(jax.random.fold_in(key, 23), -6.0, 6.0, (EXPERTS, D, width), jnp.float32)
    base = base * D ** (-0.5)
    device_range = jnp.arange(EXPERTS, dtype=jnp.int32)
    same_earlier = (spare[None, :] == spare[:, None]) & (device_range[None, :] < device_range[:, None])
    holder_rank = jnp.sum(same_earlier.astype(jnp.int32), axis=1)
    third_index = holder_rank % 3
    safe_expert = jnp.maximum(spare, 0)
    owner = jnp.sum(jnp.where(device_range[None, :] == safe_expert[:, None], home[None, :], 0), axis=1).astype(jnp.int32)
    within = jnp.arange(third_width, dtype=jnp.int32)
    start_col = third_index[:, None] * third_width + within[None, :]
    columns = jnp.concatenate([start_col, start_col + FF, start_col + 2 * FF], axis=1).astype(jnp.int32)
    row_range = jnp.arange(D, dtype=jnp.int32)
    copied = base[owner[:, None, None], row_range[None, :, None], columns[:, None, :]]
    return jnp.concatenate([base, copied], axis=2).astype(jnp.bfloat16)


def block_scale(key, extent, split, low, top_value):
    loudness, own = 1.0, jax.random.fold_in(key, 6)
    for dim, blocks in split:
        draws = jnp.exp(jax.random.uniform(jax.random.fold_in(own, dim), (blocks,), jnp.float32, low / len(split), top_value / len(split)))
        loudness = loudness * jnp.repeat(draws, extent[dim] // blocks).reshape([-1 if axis == dim else 1 for axis in range(len(extent))])
    return loudness


def noise(key, dims, scale, bound, cuts=(), held_as=jnp.bfloat16):
    result = scale * jax.random.normal(key, dims, jnp.float32)
    if cuts:
        result = result * block_scale(key, dims, cuts, -0.22, 0.18)
    return jnp.clip(result, -bound, bound).astype(held_as)


def setup_inputs(seed: int = 0, part: int = 0) -> dict:
    arg_keys = jax.random.split(jax.random.key(seed), 7)
    part_keys = jax.random.split(jax.random.fold_in(arg_keys[6], part), 7)
    return {
        "tokens": noise(part_keys[0], (TOKENS, D), 1.0, 6.0, ((0, 16),)),
        "expert_ids": draw_expert_ids(jax.random.fold_in(jax.random.fold_in(arg_keys[6], part), 71), part),
        "gate_values": jnp.clip(0.1 + 0.9 * jax.random.uniform(part_keys[2], (TOKENS, TOP), jnp.float32) ** block_scale(part_keys[2], (TOKENS, TOP), ((0, 16),), -0.2, 0.2), 0.1, 1.0),
        "expert_weights": draw_expert_weights(jax.random.fold_in(jax.random.fold_in(arg_keys[6], part), 71), part),
        "home_slot": draw_home_slot(jax.random.fold_in(jax.random.fold_in(arg_keys[6], part), 71), part),
        "spare_expert": draw_spare_expert(jax.random.fold_in(jax.random.fold_in(arg_keys[6], part), 71), part),
    }


def expert_rows(token_rows, weight_block):
    hidden_width = weight_block.shape[1] // 3
    gate_up = jnp.dot(token_rows, weight_block[:, :2 * hidden_width], preferred_element_type=jnp.float32)
    hidden = (jax.nn.silu(gate_up[:, :hidden_width]) * gate_up[:, hidden_width:]).astype(jnp.bfloat16)
    answer = lax.dot_general(hidden, weight_block[:, 2 * hidden_width:], (((1,), (1,)), ((), ())), preferred_element_type=jnp.float32)
    return answer.astype(jnp.bfloat16)


def host_tables(expert_ids, home_slot, spare_expert):
    devices = N_EP
    per_device = TOK_DEV * TOP
    ids_grid = expert_ids.reshape(devices, per_device).astype(jnp.int32)
    expert_range = jnp.arange(EXPERTS, dtype=jnp.int32)
    holders = (spare_expert[None, :] == expert_range[:, None]).astype(jnp.int32)
    copies = 1 + jnp.sum(holders, axis=1) // 3
    holder_rank = jnp.cumsum(holders, axis=1)
    chosen = (ids_grid[:, :, None] == expert_range[None, None, :]).astype(jnp.int32)
    earlier = jnp.cumsum(chosen, axis=1) - chosen
    arrival = jnp.sum(earlier * chosen, axis=2)
    copy_count = copies[ids_grid]
    copy_index = arrival % copy_count
    position = arrival // copy_count
    first_rank = 3 * copy_index - 2
    matched = (holders[ids_grid] == 1) & (holder_rank[ids_grid] == first_rank[:, :, None])
    device_range = jnp.arange(devices, dtype=jnp.int32)
    spare_device = jnp.sum(jnp.where(matched, device_range[None, None, :], 0), axis=2).astype(jnp.int32)
    host = jnp.where(copy_index == 0, 2 * home_slot[ids_grid], 2 * spare_device + 1)
    host = jnp.where(position < CAP, host, 2 * devices).astype(jnp.int32)
    column = (device_range[:, None] * CAP + position).astype(jnp.int32)
    assignment = jnp.arange(devices * per_device, dtype=jnp.int32).reshape(devices, per_device)
    table = jnp.full((2 * devices, devices * CAP), -1, dtype=jnp.int32)
    return table.at[host, column].set(assignment, mode="drop")


def reference(tokens, expert_ids, gate_values, expert_weights, home_slot, spare_expert):
    table = host_tables(expert_ids, home_slot, spare_expert)
    flat_gates = gate_values.reshape(-1)
    expert_range = jnp.arange(EXPERTS, dtype=jnp.int32)

    def one_host(total, host):
        device = (host // 2).astype(jnp.int32)
        spare_home = jnp.sum(jnp.where(expert_range == spare_expert[device], home_slot, 0)).astype(jnp.int32)
        block_index = jnp.where(host % 2 == 0, device, spare_home).astype(jnp.int32)
        weight_block = lax.dynamic_index_in_dim(expert_weights, block_index, 0, keepdims=False)[:, :3 * FF]
        entries = table[host]
        valid = entries >= 0
        safe_entries = jnp.where(valid, entries, 0).astype(jnp.int32)
        token_index = (safe_entries // TOP).astype(jnp.int32)
        answers = expert_rows(tokens[token_index], weight_block)
        scaling = jnp.where(valid, flat_gates[safe_entries], jnp.zeros_like(flat_gates[safe_entries]))
        total = total.at[token_index].add(answers.astype(jnp.float32) * scaling[:, None])
        return total, None

    start_total = jnp.zeros((TOKENS, D), dtype=jnp.float32)
    total, unused = lax.scan(one_host, start_total, jnp.arange(2 * N_EP, dtype=jnp.int32))
    return total.astype(jnp.bfloat16)
```

```python
import jax
import jax.numpy as jnp
from jax import lax
from jax.sharding import PartitionSpec as P


def device_gates(expert_ids, gate_values, home_slot, spare_expert, capacity):
    count = home_slot.shape[0]
    span = jnp.arange(count, dtype=jnp.int32)
    expert_of = jnp.sum(jnp.where(home_slot[None, :] == span[:, None], span[None, :], 0), axis=1)
    thirds = jnp.sum((spare_expert[None, :] == expert_of[:, None]).astype(jnp.int32), axis=1)
    limit = capacity * (1 + thirds // 3)
    match = expert_ids[:, :, None] == expert_of[None, None, :]
    gates = jnp.sum(jnp.where(match, gate_values[:, :, None], 0.0), axis=1)
    named = jnp.any(match, axis=1)
    rows = jnp.arange(expert_ids.shape[0], dtype=jnp.int32)
    before = (rows[None, :] < rows[:, None]).astype(jnp.bfloat16)
    arrival = jnp.dot(before, named.astype(jnp.bfloat16), preferred_element_type=jnp.float32)
    return jnp.where(named & (arrival < limit[None, :].astype(jnp.float32)), gates, 0.0)


def shards(tokens, expert_ids, gate_values, expert_weights, home_slot, spare_expert):
    devices = lax.axis_size("ep")
    me = lax.axis_index("ep")
    local_tokens, feature = tokens.shape
    capacity = local_tokens * expert_ids.shape[1] // devices
    width = expert_weights.shape[2] // 4
    block = expert_weights[0, :, : 3 * width]
    gates = device_gates(expert_ids, gate_values, home_slot, spare_expert, capacity)
    everything = lax.all_gather(tokens, "ep", axis=0, tiled=True)
    gates_all = lax.all_gather(gates, "ep", axis=0, tiled=True)
    mine = lax.dynamic_slice_in_dim(gates_all, me, 1, axis=1)
    gate_up = jnp.dot(everything, block[:, : 2 * width], preferred_element_type=jnp.float32)
    hidden = (jax.nn.silu(gate_up[:, :width]) * gate_up[:, width:]).astype(jnp.bfloat16)
    answer = lax.dot_general(
        hidden, block[:, 2 * width :], (((1,), (1,)), ((), ())), preferred_element_type=jnp.float32
    )
    weighted = jnp.where(mine > 0, answer * mine, 0.0).astype(jnp.bfloat16)
    return lax.psum_scatter(weighted, "ep", scatter_dimension=0, tiled=True).astype(jnp.bfloat16)


def solution(mesh):
    in_specs = (
        P(("groups", "ep"), None),
        P(("groups", "ep"), None),
        P(("groups", "ep"), None),
        P(("groups", "ep"), None, None),
        P("groups"),
        P("groups"),
    )
    out_specs = P(("groups", "ep"), None)
    return jax.shard_map(shards, mesh=mesh, in_specs=in_specs, out_specs=out_specs, check_vma=False)
```

```python
import functools

import jax
import jax.numpy as jnp
from jax import lax
from jax.experimental import pallas as pl
from jax.experimental.pallas import tpu as pltpu
from jax.sharding import PartitionSpec as P


def device_gates(expert_ids, gate_values, home_slot, spare_expert, capacity):
    count = home_slot.shape[0]
    span = jnp.arange(count, dtype=jnp.int32)
    expert_of = jnp.sum(jnp.where(home_slot[None, :] == span[:, None], span[None, :], 0), axis=1)
    thirds = jnp.sum((spare_expert[None, :] == expert_of[:, None]).astype(jnp.int32), axis=1)
    limit = capacity * (1 + thirds // 3)
    match = expert_ids[:, :, None] == expert_of[None, None, :]
    gates = jnp.sum(jnp.where(match, gate_values[:, :, None], 0.0), axis=1)
    named = jnp.any(match, axis=1)
    rows = jnp.arange(expert_ids.shape[0], dtype=jnp.int32)
    before = (rows[None, :] < rows[:, None]).astype(jnp.bfloat16)
    arrival = jnp.dot(before, named.astype(jnp.bfloat16), preferred_element_type=jnp.float32)
    return jnp.where(named & (arrival < limit[None, :].astype(jnp.float32)), gates, 0.0)


MESH = pl.DeviceIdType.MESH


def fused(devices, feature, width, x_ref, w_hbm, out_ref, xall, w, hid, part, sib_out, sib_in, rs,
          w_sem, ag_send, ag_recv, sx_send, sx_recv, sr_send, sr_recv, rs_send, rs_recv):
    chips = devices // 2
    far = chips // 2
    me = lax.axis_index("ep")
    core = me % 2
    chip = me // 2
    odd = chip % 2
    place = (1 - odd) * (chip // 2) + odd * (chips - 1 - chip // 2)

    def device_at(spot):
        low = 1 - spot // far
        return 2 * (low * 2 * spot + (1 - low) * (2 * (chips - 1 - spot) + 1)) + core

    right = device_at((place + 1) % chips)
    left = device_at((place + chips - 1) % chips)
    sibling = me + 1 - 2 * core
    toward = (right, left)

    def remote(src, dst, send, recv, device):
        return pltpu.make_async_remote_copy(src_ref=src, dst_ref=dst, send_sem=send, recv_sem=recv,
                                            device_id={"ep": device}, device_id_type=MESH)

    def gather(side, d, half):
        src_side = 0 if isinstance(d, int) and d == 0 else side
        dst_side = 0 if side == 0 else 1 - (d + 1) // far
        return remote(xall.at[d, src_side, core, half], xall.at[d + 1, dst_side, core, half],
                      ag_send.at[side, d, half], ag_recv.at[side, d + 1, half], toward[side])

    def share(side, d, half):
        slot = xall.at[d, side, core, half]
        return remote(slot, slot, sx_send.at[side, d, half], sx_recv.at[side, d, half], sibling)

    def exchange(slot, side, d):
        return remote(sib_out.at[slot, side], sib_in.at[d, side],
                      sr_send.at[slot, side], sr_recv.at[d, side], sibling)

    def reduce(way, d, half):
        return remote(rs.at[way, d, half], rs.at[way, d - 1, half],
                      rs_send.at[way, d, half], rs_recv.at[way, d - 1, half], toward[1 - way])

    def up(d, sides):
        rows = sides * 2 * x_ref.shape[0] * x_ref.shape[1]
        tile = 256

        @pl.loop(0, width // tile)
        def _(f):
            x = xall[d, :sides, :, :, :, :feature].reshape(rows, feature)
            at = pl.multiple_of(f * tile, tile)
            gate = jnp.dot(x, w[:, pl.ds(at, tile)], preferred_element_type=jnp.float32)
            lift = jnp.dot(x, w[:, pl.ds(width + at, tile)], preferred_element_type=jnp.float32)
            hid[:rows, pl.ds(at, tile)] = (gate * lax.logistic(gate) * lift).astype(jnp.bfloat16)

    def down(d, sides, slot):
        half_rows = x_ref.shape[1]
        rows = sides * 4 * half_rows
        extra = xall[d, :sides, :, :, :, feature:].reshape(rows, -1).astype(jnp.float32)
        lane = lax.broadcasted_iota(jnp.int32, extra.shape, 1)
        gates = jnp.sum(jnp.where((lane == me) | (lane == me + devices), extra, 0.0), axis=1, keepdims=True)
        tile = 512

        @pl.loop(0, feature // tile)
        def _(o):
            at = pl.multiple_of(o * tile, tile)
            answer = lax.dot_general(hid[:rows], w[pl.ds(at, tile), 2 * width:],
                                     (((1,), (1,)), ((), ())), preferred_element_type=jnp.float32)
            answer = answer.astype(jnp.bfloat16).astype(jnp.float32)
            value = jnp.where(gates > 0, answer * gates, 0.0).reshape(sides, 2, 2, half_rows, tile)
            mine = jnp.where(core == 0, value[:, 0], value[:, 1])
            other = jnp.where(core == 0, value[:, 1], value[:, 0])
            part[d, :sides, :, :, pl.ds(at, tile)] = mine.astype(part.dtype)
            sib_out[slot, :sides, :, :, pl.ds(at, tile)] = other.astype(jnp.bfloat16)

        for side in range(sides):
            exchange(slot, side, d).start()

    def total(side, d, half):
        return part[d, side, half].astype(jnp.float32) + sib_in[d, side, half].astype(jnp.float32)

    def pass_on(way, d, half):
        reduce(way, d + 1, half).wait_recv()
        rs[way, d, half] = (total(way, d, half) + rs[way, d, half].astype(jnp.float32)).astype(jnp.bfloat16)
        reduce(way, d, half).start()

    weights = pltpu.make_async_copy(w_hbm.at[0, :, pl.ds(0, 3 * width)], w, w_sem)
    weights.start()
    xall[0, 0, core] = x_ref[...]
    barrier = pltpu.get_barrier_semaphore()
    for device in (right, left, sibling):
        pl.semaphore_signal(barrier, inc=1, device_id={"ep": device}, device_id_type=MESH)
    pl.semaphore_wait(barrier, 3)

    for turn in range(2):
        for side in range(2):
            gather(side, 0, turn if side == 0 else 1 - turn).start()
        share(0, 0, turn).start()
    for half in range(2):
        share(0, 0, half).wait_recv()
    weights.wait()
    up(0, 1)
    for side in range(2):
        gather(side, 0, side).wait_recv()
        gather(side, 1, side).start()
        share(side, 1, side).start()
    down(0, 1, 2)
    for side in range(2):
        gather(side, 0, 1 - side).wait_recv()
        gather(side, 1, 1 - side).start()
        share(side, 1, 1 - side).start()

    @pl.loop(2, far + 1)
    def _(d):
        last = d // far
        for side in range(2):
            gather(side, d - 1, side).wait_recv()

        @pl.when(last == 0)
        def _():
            for side in range(2):
                gather(side, d, side).start()
                share(side, d, side).start()

        @pl.when(last == 1)
        def _():
            for half in range(2):
                share(0, far, half).start()

        for side in range(2):
            for half in range(2):
                share(side, d - 1, half).wait_recv()
        up(d - 1, 2)

        @pl.when(last == 0)
        def _():
            for side in range(2):
                gather(side, d - 1, 1 - side).wait_recv()

                @pl.when(d < far - 1)
                def _():
                    gather(side, d, 1 - side).start()
                share(side, d, 1 - side).start()

        @pl.when(d >= 4)
        def _():
            for side in range(2):
                exchange((d - 1) % 2, side, d - 3).wait_send()
        down(d - 1, 2, (d - 1) % 2)

    for half in range(2):
        share(0, far, half).wait_recv()
    up(far, 1)
    for side in range(2):
        exchange((far - 1) % 2, side, far - 1).wait_recv()
    for way in range(2):
        half = way
        rs[way, far - 1, half] = total(way, far - 1, half).astype(jnp.bfloat16)
        reduce(way, far - 1, half).start()
    down(far, 1, 3)
    exchange(3, 0, far).wait_recv()
    for way in range(2):
        half = 1 - way
        rs[way, far, half] = total(0, far, half).astype(jnp.bfloat16)
        reduce(way, far, half).start()

    @pl.loop(1, far - 1)
    def _(back):
        d = far - back
        for side in range(2):
            exchange(0, side, d - 1).wait_recv()
        for way in range(2):
            pass_on(way, d - 1, way)
        for way in range(2):
            pass_on(way, d, 1 - way)

    for way in range(2):
        pass_on(way, 1, 1 - way)
    exchange(2, 0, 0).wait_recv()
    for half in range(2):
        for way in range(2):
            reduce(way, 1, half).wait_recv()
        out_ref[half] = (total(0, 0, half) + rs[0, 0, half].astype(jnp.float32)
                         + rs[1, 0, half].astype(jnp.float32)).astype(out_ref.dtype)

    for half in range(2):
        share(0, 0, half).wait_send()
        share(0, far, half).wait_send()
        for side in range(2):
            gather(side, 0, half).wait_send()
    for side in range(2):
        gather(side, far - 1, side).wait_send()
        share(side, far - 1, 0).wait_send()
        share(side, far - 1, 1).wait_send()
        exchange((far - 1) % 2, side, far - 1).wait_send()
        exchange((far - 2) % 2, side, far - 2).wait_send()
        reduce(side, far, 1 - side).wait_send()
    exchange(2, 0, 0).wait_send()
    exchange(3, 0, far).wait_send()

    @pl.loop(1, far - 1)
    def _(d):
        for side in range(2):
            for half in range(2):
                gather(side, d, half).wait_send()
                share(side, d, half).wait_send()

    @pl.loop(1, far)
    def _(d):
        for way in range(2):
            for half in range(2):
                reduce(way, d, half).wait_send()


def shards(tokens, expert_ids, gate_values, expert_weights, home_slot, spare_expert):
    devices = lax.axis_size("ep")
    local_tokens, feature = tokens.shape
    capacity = local_tokens * expert_ids.shape[1] // devices
    width = expert_weights.shape[2] // 4
    gates = device_gates(expert_ids, gate_values, home_slot, spare_expert, capacity)
    high = lax.reduce_precision(gates, 8, 7)
    extra = jnp.concatenate([high, gates - high], axis=1).astype(jnp.bfloat16)
    extra = jnp.pad(extra, ((0, 0), (0, -extra.shape[1] % 128)))
    half_rows = local_tokens // 2
    x = jnp.concatenate([tokens, extra], axis=1).reshape(2, half_rows, -1)
    far = devices // 4
    kept = jnp.float32 if devices <= 16 else jnp.bfloat16
    dma = pltpu.SemaphoreType.DMA
    result = pl.pallas_call(
        functools.partial(fused, devices, feature, width),
        out_shape=jax.ShapeDtypeStruct((2, half_rows, feature), jnp.bfloat16),
        in_specs=[pl.BlockSpec(memory_space=pltpu.VMEM), pl.BlockSpec(memory_space=pl.ANY)],
        out_specs=pl.BlockSpec(memory_space=pltpu.VMEM),
        scratch_shapes=[
            pltpu.VMEM((far + 1, 2, 2) + x.shape, jnp.bfloat16),
            pltpu.VMEM((feature, 3 * width), jnp.bfloat16),
            pltpu.VMEM((4 * local_tokens, width), jnp.bfloat16),
            pltpu.VMEM((far + 1, 2, 2, half_rows, feature), kept),
            pltpu.VMEM((4, 2, 2, half_rows, feature), jnp.bfloat16),
            pltpu.VMEM((far + 1, 2, 2, half_rows, feature), jnp.bfloat16),
            pltpu.VMEM((2, far + 1, 2, half_rows, feature), jnp.bfloat16),
            dma,
            dma((2, far + 1, 2)),
            dma((2, far + 1, 2)),
            dma((2, far + 1, 2)),
            dma((2, far + 1, 2)),
            dma((4, 2)),
            dma((far + 1, 2)),
            dma((2, far + 1, 2)),
            dma((2, far + 1, 2)),
        ],
        compiler_params=pltpu.CompilerParams(
            collective_id=0, has_side_effects=True, vmem_limit_bytes=(44 if devices <= 16 else 62) * 2**20
        ),
    )(x, expert_weights)
    return result.reshape(local_tokens, feature)


def solution(mesh):
    in_specs = (
        P(("groups", "ep"), None),
        P(("groups", "ep"), None),
        P(("groups", "ep"), None),
        P(("groups", "ep"), None, None),
        P("groups"),
        P("groups"),
    )
    out_specs = P(("groups", "ep"), None)
    return jax.shard_map(shards, mesh=mesh, in_specs=in_specs, out_specs=out_specs, check_vma=False)
```

```python
import functools

import jax
import jax.numpy as jnp
from jax import lax
from jax.experimental import pallas as pl
from jax.experimental.pallas import tpu as pltpu
from jax.sharding import PartitionSpec as P


MESH = pl.DeviceIdType.MESH


def fused(devices, feature, width, capacity, home, spare, ids_hbm, gate_hbm, x_hbm, w_hbm, out_ref,
          xall, w, ids_ref, gate_ref, hid, part, sib_out, sib_in, near, back, in_sem, ga_send, ga_recv,
          sh_send, sh_recv, ex_send, ex_recv, re_send, re_recv):
    chips = devices // 2
    far = chips // 2
    me = lax.axis_index("ep")
    core = me % 2
    chip = me // 2
    odd = chip % 2
    place = (1 - odd) * (chip // 2) + odd * (chips - 1 - chip // 2)

    def device_at(spot):
        low = 1 - spot // far
        return 2 * (low * 2 * spot + (1 - low) * (2 * (chips - 1 - spot) + 1)) + core

    right = device_at((place + 1) % chips)
    left = device_at((place + chips - 1) % chips)
    sibling = me + 1 - 2 * core
    toward = (right, left)

    def remote(src, dst, send, recv, device):
        return pltpu.make_async_remote_copy(src_ref=src, dst_ref=dst, send_sem=send, recv_sem=recv,
                                            device_id={"ep": device}, device_id_type=MESH)

    def gather(kind, d, side):
        flip = 1 - side if kind == 1 and isinstance(d, int) and d == 0 else side
        first = 0 if isinstance(d, int) and d == 0 else kind * far
        return remote(xall.at[first + d, flip, core], xall.at[kind * far + d + 1, side, core],
                      ga_send.at[kind, d, side], ga_recv.at[kind, d + 1, side], toward[side])

    def share(block, side):
        slot = xall.at[block, side, core]
        return remote(slot, slot, sh_send.at[block, side], sh_recv.at[block, side], sibling)

    def exchange(block):
        return remote(sib_out.at[block % sib_out.shape[0]], sib_in.at[block],
                      ex_send.at[block], ex_recv.at[block], sibling)

    sums = (near, back)

    def reduce(kind, d, way):
        return remote(sums[kind].at[d, way], sums[kind].at[d - 1, way],
                      re_send.at[kind, d, way], re_recv.at[kind, d - 1, way], toward[1 - way])

    half_rows = x_hbm.shape[1]
    rows = 4 * half_rows

    def compute(block):
        for side in range(2):
            share(block, side).wait_recv()
        tile = 256

        @pl.loop(0, width // tile, unroll=True)
        def _(f):
            x = xall[block, :, :, :, :feature].reshape(rows, feature)
            at = pl.multiple_of(f * tile, tile)
            gate = jnp.dot(x, w[:, pl.ds(at, tile)], preferred_element_type=jnp.float32)
            lift = jnp.dot(x, w[:, pl.ds(width + at, tile)], preferred_element_type=jnp.float32)
            hid[:, pl.ds(at, tile)] = (gate * lax.logistic(gate) * lift).astype(jnp.bfloat16)

        extra = xall[block, :, :, :, feature:].reshape(rows, -1).astype(jnp.float32)
        gates = jnp.sum(jnp.where(at_home == me, extra, 0.0), axis=1, keepdims=True)
        ring = sib_out.shape[0]
        if 2 * far > ring:

            @pl.when(block >= ring)
            def _():
                exchange(block - ring).wait_send()

        span = 512

        @pl.loop(0, feature // span, unroll=True)
        def _(o):
            at = pl.multiple_of(o * span, span)
            answer = lax.dot_general(hid[...], w[pl.ds(at, span), 2 * width:],
                                     (((1,), (1,)), ((), ())), preferred_element_type=jnp.float32)
            answer = answer.astype(jnp.bfloat16).astype(jnp.float32)
            value = jnp.where(gates > 0, answer * gates, 0.0).reshape(2, 2, half_rows, span)
            mine = jnp.where(core == 0, value[:, 0], value[:, 1])
            other = jnp.where(core == 0, value[:, 1], value[:, 0])
            part[block, :, :, pl.ds(at, span)] = mine.astype(part.dtype)
            sib_out[block % ring, :, :, pl.ds(at, span)] = other.astype(jnp.bfloat16)

        exchange(block).start()

    def total(block, side):
        return part[block, side].astype(jnp.float32) + sib_in[block, side].astype(jnp.float32)

    def begin(kind, d):
        exchange(kind * far + d).wait_recv()
        for way in range(2):
            sums[kind][d, way] = total(kind * far + d, way).astype(jnp.bfloat16)
            reduce(kind, d, way).start()

    def pass_on(kind, d):
        exchange(kind * far + d).wait_recv()
        for way in range(2):
            reduce(kind, d + 1, way).wait_recv()
            held = sums[kind][d, way].astype(jnp.float32)
            sums[kind][d, way] = (total(kind * far + d, way) + held).astype(jnp.bfloat16)
            reduce(kind, d, way).start()

    fetches = [
        pltpu.make_async_copy(ids_hbm, ids_ref, in_sem.at[0]),
        pltpu.make_async_copy(gate_hbm, gate_ref, in_sem.at[1]),
        pltpu.make_async_copy(x_hbm, xall.at[0, :, core, :, pl.ds(0, feature)], in_sem.at[2]),
        pltpu.make_async_copy(w_hbm.at[0, :, pl.ds(0, 3 * width)], w, in_sem.at[3]),
    ]
    for fetch in fetches:
        fetch.start()
    barrier = pltpu.get_barrier_semaphore()
    for device in (right, left, sibling):
        pl.semaphore_signal(barrier, inc=1, device_id={"ep": device}, device_id_type=MESH)

    own_rows, lanes = ids_ref.shape[0], xall.shape[-1] - feature
    lane_row = lax.broadcasted_iota(jnp.int32, (1, lanes), 1)
    expert_row = jnp.where(lane_row < 2 * devices, lane_row % devices, -2)
    thirds = jnp.zeros((1, lanes), jnp.int32)
    at_home = jnp.full((1, lanes), -1, jnp.int32)
    for e in range(devices):
        thirds = thirds + jnp.where(expert_row == spare[e], 1, 0)
        at_home = jnp.where(expert_row == e, home[e], at_home)
    limit = capacity * jnp.where(thirds >= 6, 3, jnp.where(thirds >= 3, 2, 1))
    fetches[0].wait()
    fetches[1].wait()
    gates = jnp.zeros((own_rows, lanes), jnp.float32)
    for k in range(ids_ref.shape[1]):
        gates = gates + jnp.where(ids_ref[:, k : k + 1] == expert_row, gate_ref[:, k : k + 1], 0.0)
    named = jnp.where(gates > 0, 1.0, 0.0).astype(jnp.bfloat16)
    earlier = lax.broadcasted_iota(jnp.int32, (own_rows, own_rows), 1) < lax.broadcasted_iota(
        jnp.int32, (own_rows, own_rows), 0)
    arrival = jnp.dot(jnp.where(earlier, 1.0, 0.0).astype(jnp.bfloat16), named, preferred_element_type=jnp.float32)
    gates = jnp.where(arrival < limit.astype(jnp.float32), gates, 0.0)
    high = gates.astype(jnp.bfloat16)
    rest = gates - high.astype(jnp.float32)
    extra = jnp.where(lane_row < devices, high.astype(jnp.float32), rest).astype(jnp.bfloat16)
    xall[0, :, core, :, feature:] = extra.reshape(2, own_rows // 2, lanes)
    fetches[2].wait()
    pl.semaphore_wait(barrier, 3)

    for side in range(2):
        gather(0, 0, side).start()
    for side in range(2):
        share(0, side).start()
    fetches[3].wait()
    for side in range(2):
        gather(0, 0, side).wait_send()
    for side in range(2):
        gather(1, 0, side).start()

    @pl.loop(1, far + 1)
    def _(d):
        for side in range(2):
            gather(0, d - 1, side).wait_recv()

            @pl.when(d < far)
            def _():
                gather(0, d, side).start()

        for side in range(2):
            share(d, side).start()

        @pl.when(d == far - 1)
        def _():
            for side in range(2):
                gather(1, 0, side).wait_recv()
                gather(1, 1, side).start()
                share(far + 1, side).start()

        compute(d - 1)

    compute(far)

    @pl.loop(2, far)
    def _(d):
        for side in range(2):
            gather(1, d - 1, side).wait_recv()

            @pl.when(d < far - 1)
            def _():
                gather(1, d, side).start()

            share(far + d, side).start()

        @pl.when(d == 2)
        def _():
            begin(0, far)

        compute(far + d - 1)

    pass_on(0, far - 1)
    compute(2 * far - 1)
    begin(1, far - 1)

    @pl.loop(2, far)
    def _(step):
        pass_on(0, far - step)
        pass_on(1, far - step)

    exchange(0).wait_recv()
    for half in range(2):
        reduce(0, 1, half).wait_recv()
        reduce(1, 1, 1 - half).wait_recv()
        out_ref[half] = (total(0, half) + near[0, half].astype(jnp.float32)
                         + back[0, 1 - half].astype(jnp.float32)).astype(out_ref.dtype)

    @pl.loop(0, 2 * far)
    def _(block):
        for side in range(2):
            share(block, side).wait_send()

    @pl.loop(max(0, 2 * far - sib_out.shape[0]), 2 * far)
    def _(block):
        exchange(block).wait_send()

    for side in range(2):
        gather(1, 0, side).wait_send()
        gather(0, far - 1, side).wait_send()
        reduce(0, far, side).wait_send()
        reduce(0, far - 1, side).wait_send()
        reduce(1, far - 1, side).wait_send()

    @pl.loop(1, far - 1)
    def _(d):
        for side in range(2):
            for kind in range(2):
                gather(kind, d, side).wait_send()
                reduce(kind, d, side).wait_send()


def shards(tokens, expert_ids, gate_values, expert_weights, home_slot, spare_expert):
    devices = lax.axis_size("ep")
    local_tokens, feature = tokens.shape
    capacity = local_tokens * expert_ids.shape[1] // devices
    width = expert_weights.shape[2] // 4
    half_rows = local_tokens // 2
    lanes = pl.cdiv(2 * devices, 128) * 128
    x = tokens.reshape(2, half_rows, feature)
    far = devices // 4
    kept = jnp.float32 if devices <= 16 else jnp.bfloat16
    dma = pltpu.SemaphoreType.DMA
    result = pl.pallas_call(
        functools.partial(fused, devices, feature, width, capacity),
        out_shape=jax.ShapeDtypeStruct((2, half_rows, feature), jnp.bfloat16),
        in_specs=[pl.BlockSpec(memory_space=pltpu.SMEM)] * 2 + [pl.BlockSpec(memory_space=pl.ANY)] * 4,
        out_specs=pl.BlockSpec(memory_space=pltpu.VMEM),
        scratch_shapes=[
            pltpu.VMEM((2 * far, 2, 2, half_rows, feature + lanes), jnp.bfloat16),
            pltpu.VMEM((feature, 3 * width), jnp.bfloat16),
            pltpu.VMEM(expert_ids.shape, jnp.int32),
            pltpu.VMEM(gate_values.shape, jnp.float32),
            pltpu.VMEM((2 * local_tokens, width), jnp.bfloat16),
            pltpu.VMEM((2 * far, 2, half_rows, feature), kept),
            pltpu.VMEM((8, 2, half_rows, feature), jnp.bfloat16),
            pltpu.VMEM((2 * far, 2, half_rows, feature), jnp.bfloat16),
            pltpu.VMEM((far + 1, 2, half_rows, feature), jnp.bfloat16),
            pltpu.VMEM((far, 2, half_rows, feature), jnp.bfloat16),
            dma((4,)),
            dma((2, far + 1, 2)),
            dma((2, far + 1, 2)),
            dma((2 * far, 2)),
            dma((2 * far, 2)),
            dma((2 * far,)),
            dma((2 * far,)),
            dma((2, far + 1, 2)),
            dma((2, far + 1, 2)),
        ],
        compiler_params=pltpu.CompilerParams(
            collective_id=0, has_side_effects=True, vmem_limit_bytes=(44 if devices <= 16 else 62) * 2**20
        ),
    )(home_slot, spare_expert, expert_ids, gate_values, x, expert_weights)
    return result.reshape(local_tokens, feature)


def solution(mesh):
    in_specs = (
        P(("groups", "ep"), None),
        P(("groups", "ep"), None),
        P(("groups", "ep"), None),
        P(("groups", "ep"), None, None),
        P("groups"),
        P("groups"),
    )
    out_specs = P(("groups", "ep"), None)
    return jax.shard_map(shards, mesh=mesh, in_specs=in_specs, out_specs=out_specs, check_vma=False)
```

```python
import functools

import jax
import jax.numpy as jnp
from jax import lax
from jax.experimental import pallas as pl
from jax.experimental.pallas import tpu as pltpu
from jax.sharding import PartitionSpec as P


MESH = pl.DeviceIdType.MESH


def fused(devices, feature, width, capacity, home, spare, ids_hbm, gate_hbm, x_hbm, w_hbm, out_ref,
          xall, w, ids_ref, gate_ref, hid, part, sib_out, sib_in, near, back, in_sem, ga_send, ga_recv,
          sh_send, sh_recv, ex_send, ex_recv, re_send, re_recv):
    chips = devices // 2
    far = chips // 2
    me = lax.axis_index("ep")
    core = me % 2
    chip = me // 2
    odd = chip % 2
    place = (1 - odd) * (chip // 2) + odd * (chips - 1 - chip // 2)

    def device_at(spot):
        low = 1 - spot // far
        return 2 * (low * 2 * spot + (1 - low) * (2 * (chips - 1 - spot) + 1)) + core

    right = device_at((place + 1) % chips)
    left = device_at((place + chips - 1) % chips)
    sibling = me + 1 - 2 * core
    toward = (right, left)

    def remote(src, dst, send, recv, device):
        return pltpu.make_async_remote_copy(src_ref=src, dst_ref=dst, send_sem=send, recv_sem=recv,
                                            device_id={"ep": device}, device_id_type=MESH)

    def gather(kind, d, side):
        flip = 1 - side if kind == 1 and isinstance(d, int) and d == 0 else side
        first = 0 if isinstance(d, int) and d == 0 else kind * far
        return remote(xall.at[first + d, flip, core], xall.at[kind * far + d + 1, side, core],
                      ga_send.at[kind, d, side], ga_recv.at[kind, d + 1, side], toward[side])

    def share(block, side):
        slot = xall.at[block, side, core]
        return remote(slot, slot, sh_send.at[block, side], sh_recv.at[block, side], sibling)

    def exchange(block):
        return remote(sib_out.at[block % sib_out.shape[0]], sib_in.at[block],
                      ex_send.at[block], ex_recv.at[block], sibling)

    sums = (near, back)

    def reduce(kind, d, way):
        return remote(sums[kind].at[d, way], sums[kind].at[d - 1, way],
                      re_send.at[kind, d, way], re_recv.at[kind, d - 1, way], toward[1 - way])

    half_rows = x_hbm.shape[1]
    rows = 4 * half_rows

    def compute(block):
        for side in range(2):
            share(block, side).wait_recv()
        tile = 256

        @pl.loop(0, width // tile)
        def _(f):
            x = xall[block, :, :, :, :feature].reshape(rows, feature)
            at = pl.multiple_of(f * tile, tile)
            gate = jnp.dot(x, w[:, pl.ds(at, tile)], preferred_element_type=jnp.float32)
            lift = jnp.dot(x, w[:, pl.ds(width + at, tile)], preferred_element_type=jnp.float32)
            hid[:, pl.ds(at, tile)] = (gate * lax.logistic(gate) * lift).astype(jnp.bfloat16)

        extra = xall[block, :, :, :, feature:].reshape(rows, -1).astype(jnp.float32)
        gates = jnp.sum(jnp.where(at_home == me, extra, 0.0), axis=1, keepdims=True)
        ring = sib_out.shape[0]
        if 2 * far > ring:

            @pl.when(block >= ring)
            def _():
                exchange(block - ring).wait_send()

        span = 512

        @pl.loop(0, feature // span)
        def _(o):
            at = pl.multiple_of(o * span, span)
            answer = lax.dot_general(hid[...], w[pl.ds(at, span), 2 * width:],
                                     (((1,), (1,)), ((), ())), preferred_element_type=jnp.float32)
            answer = answer.astype(jnp.bfloat16).astype(jnp.float32)
            value = jnp.where(gates > 0, answer * gates, 0.0).reshape(2, 2, half_rows, span)
            mine = jnp.where(core == 0, value[:, 0], value[:, 1])
            other = jnp.where(core == 0, value[:, 1], value[:, 0])
            part[block, :, :, pl.ds(at, span)] = mine.astype(part.dtype)
            sib_out[block % ring, :, :, pl.ds(at, span)] = other.astype(jnp.bfloat16)

        exchange(block).start()

    def total(block, side):
        return part[block, side].astype(jnp.float32) + sib_in[block, side].astype(jnp.float32)

    def begin(kind, d):
        exchange(kind * far + d).wait_recv()
        for way in range(2):
            sums[kind][d, way] = total(kind * far + d, way).astype(jnp.bfloat16)
            reduce(kind, d, way).start()

    def pass_on(kind, d):
        exchange(kind * far + d).wait_recv()
        for way in range(2):
            reduce(kind, d + 1, way).wait_recv()
            held = sums[kind][d, way].astype(jnp.float32)
            sums[kind][d, way] = (total(kind * far + d, way) + held).astype(jnp.bfloat16)
            reduce(kind, d, way).start()

    fetches = [
        pltpu.make_async_copy(ids_hbm, ids_ref, in_sem.at[0]),
        pltpu.make_async_copy(gate_hbm, gate_ref, in_sem.at[1]),
        pltpu.make_async_copy(x_hbm, xall.at[0, :, core, :, pl.ds(0, feature)], in_sem.at[2]),
        pltpu.make_async_copy(w_hbm.at[0, :, pl.ds(0, 3 * width)], w, in_sem.at[3]),
    ]
    for fetch in fetches:
        fetch.start()
    barrier = pltpu.get_barrier_semaphore()
    for device in (right, left, sibling):
        pl.semaphore_signal(barrier, inc=1, device_id={"ep": device}, device_id_type=MESH)

    own_rows, lanes = ids_ref.shape[1], xall.shape[-1] - feature
    lane_row = lax.broadcasted_iota(jnp.int32, (1, lanes), 1)
    expert_row = jnp.where(lane_row < 2 * devices, lane_row % devices, -2)
    thirds = jnp.zeros((1, lanes), jnp.int32)
    at_home = jnp.full((1, lanes), -1, jnp.int32)
    for e in range(devices):
        thirds = thirds + jnp.where(expert_row == spare[e], 1, 0)
        at_home = jnp.where(expert_row == e, home[e], at_home)
    limit = capacity * jnp.where(thirds >= 6, 3, jnp.where(thirds >= 3, 2, 1))
    fetches[0].wait()
    fetches[1].wait()
    gates = jnp.zeros((own_rows, lanes), jnp.float32)
    ids, weights = ids_ref[...].T, gate_ref[...].T
    for k in range(ids.shape[1]):
        gates = gates + jnp.where(ids[:, k : k + 1] == expert_row, weights[:, k : k + 1], 0.0)
    named = jnp.where(gates > 0, 1.0, 0.0).astype(jnp.bfloat16)
    earlier = lax.broadcasted_iota(jnp.int32, (own_rows, own_rows), 1) < lax.broadcasted_iota(
        jnp.int32, (own_rows, own_rows), 0)
    arrival = jnp.dot(jnp.where(earlier, 1.0, 0.0).astype(jnp.bfloat16), named, preferred_element_type=jnp.float32)
    gates = jnp.where(arrival < limit.astype(jnp.float32), gates, 0.0)
    high = gates.astype(jnp.bfloat16)
    rest = gates - high.astype(jnp.float32)
    extra = jnp.where(lane_row < devices, high.astype(jnp.float32), rest).astype(jnp.bfloat16)
    xall[0, :, core, :, feature:] = extra.reshape(2, own_rows // 2, lanes)
    fetches[2].wait()
    pl.semaphore_wait(barrier, 3)

    for side in range(2):
        gather(0, 0, side).start()
    for side in range(2):
        share(0, side).start()
    fetches[3].wait()
    for side in range(2):
        gather(0, 0, side).wait_send()
    for side in range(2):
        gather(1, 0, side).start()

    @pl.loop(1, far + 1)
    def _(d):
        for side in range(2):
            gather(0, d - 1, side).wait_recv()

            @pl.when(d < far)
            def _():
                gather(0, d, side).start()

        for side in range(2):
            share(d, side).start()

        @pl.when(d == far - 1)
        def _():
            for side in range(2):
                gather(1, 0, side).wait_recv()
                gather(1, 1, side).start()
                share(far + 1, side).start()

        compute(d - 1)

    compute(far)

    @pl.loop(2, far)
    def _(d):
        for side in range(2):
            gather(1, d - 1, side).wait_recv()

            @pl.when(d < far - 1)
            def _():
                gather(1, d, side).start()

            share(far + d, side).start()

        @pl.when(d == 2)
        def _():
            begin(0, far)

        compute(far + d - 1)

    pass_on(0, far - 1)
    compute(2 * far - 1)
    begin(1, far - 1)

    @pl.loop(2, far)
    def _(step):
        pass_on(0, far - step)
        pass_on(1, far - step)

    exchange(0).wait_recv()
    for half in range(2):
        reduce(0, 1, half).wait_recv()
        reduce(1, 1, 1 - half).wait_recv()
        out_ref[half] = (total(0, half) + near[0, half].astype(jnp.float32)
                         + back[0, 1 - half].astype(jnp.float32)).astype(out_ref.dtype)

    @pl.loop(0, 2 * far)
    def _(block):
        for side in range(2):
            share(block, side).wait_send()

    @pl.loop(max(0, 2 * far - sib_out.shape[0]), 2 * far)
    def _(block):
        exchange(block).wait_send()

    for side in range(2):
        gather(1, 0, side).wait_send()
        gather(0, far - 1, side).wait_send()
        reduce(0, far, side).wait_send()
        reduce(0, far - 1, side).wait_send()
        reduce(1, far - 1, side).wait_send()

    @pl.loop(1, far - 1)
    def _(d):
        for side in range(2):
            for kind in range(2):
                gather(kind, d, side).wait_send()
                reduce(kind, d, side).wait_send()


def shards(tokens, expert_ids, gate_values, expert_weights, home_slot, spare_expert):
    devices = lax.axis_size("ep")
    local_tokens, feature = tokens.shape
    capacity = local_tokens * expert_ids.shape[1] // devices
    width = expert_weights.shape[2] // 4
    half_rows = local_tokens // 2
    lanes = pl.cdiv(2 * devices, 128) * 128
    x = tokens.reshape(2, half_rows, feature)
    far = devices // 4
    kept = jnp.float32 if devices <= 16 else jnp.bfloat16
    dma = pltpu.SemaphoreType.DMA
    result = pl.pallas_call(
        functools.partial(fused, devices, feature, width, capacity),
        out_shape=jax.ShapeDtypeStruct((2, half_rows, feature), jnp.bfloat16),
        in_specs=[pl.BlockSpec(memory_space=pltpu.SMEM)] * 2 + [pl.BlockSpec(memory_space=pl.ANY)] * 4,
        out_specs=pl.BlockSpec(memory_space=pltpu.VMEM),
        scratch_shapes=[
            pltpu.VMEM((2 * far, 2, 2, half_rows, feature + lanes), jnp.bfloat16),
            pltpu.VMEM((feature, 3 * width), jnp.bfloat16),
            pltpu.VMEM(expert_ids.shape[::-1], jnp.int32),
            pltpu.VMEM(gate_values.shape[::-1], jnp.float32),
            pltpu.VMEM((2 * local_tokens, width), jnp.bfloat16),
            pltpu.VMEM((2 * far, 2, half_rows, feature), kept),
            pltpu.VMEM((8, 2, half_rows, feature), jnp.bfloat16),
            pltpu.VMEM((2 * far, 2, half_rows, feature), jnp.bfloat16),
            pltpu.VMEM((far + 1, 2, half_rows, feature), jnp.bfloat16),
            pltpu.VMEM((far, 2, half_rows, feature), jnp.bfloat16),
            dma((4,)),
            dma((2, far + 1, 2)),
            dma((2, far + 1, 2)),
            dma((2 * far, 2)),
            dma((2 * far, 2)),
            dma((2 * far,)),
            dma((2 * far,)),
            dma((2, far + 1, 2)),
            dma((2, far + 1, 2)),
        ],
        compiler_params=pltpu.CompilerParams(
            collective_id=0, has_side_effects=True, vmem_limit_bytes=63 * 2**20
        ),
    )(home_slot, spare_expert, expert_ids.T, gate_values.T, x, expert_weights)
    return result.reshape(local_tokens, feature)


def solution(mesh):
    in_specs = (
        P(("groups", "ep"), None),
        P(("groups", "ep"), None),
        P(("groups", "ep"), None),
        P(("groups", "ep"), None, None),
        P("groups"),
        P("groups"),
    )
    out_specs = P(("groups", "ep"), None)
    return jax.shard_map(shards, mesh=mesh, in_specs=in_specs, out_specs=out_specs, check_vma=False)
```
